512 devices in a mesh: row: 8 (over x_lo, y), col: 16 (over z), vc: 4 (over x_hi, core).
Axes of the slice: x: 4 (x_hi: 2, x_lo: 2; x = x_hi * 2 + x_lo), y: 4, z: 16, core: 2. Of those that a mesh axis runs over, the one named last changes fastest.
Arguments:
- amplitudes: bfloat16 [32, 32, 128, 128], P('row', 'col'), may hold values from -6 to 6
- factors: bfloat16 [8, 16, 256, 128, 128], P('row', 'col', 'vc'), may hold values from -0.125 to 0.125
- pno_counts: int32 [32, 32], P('row', 'col'), may hold values from 32 to 128, as said below
- pair_live: int32 [32, 32], P('row', 'col'), may hold values from 0 to 1, as said below
Outputs:
- residual_ladder: float32 [32, 32, 128, 128], P('row', 'col', 'vc')
The draws below stay inside these ranges and needn't reach their ends.
Inputs may be any that keep to these rules, and one draw needn't show every extreme that they name: pno_counts[i, j] equals pno_counts[j, i]; every diagonal entry is 128. pair_live[i, j] equals pair_live[j, i]; every diagonal entry is 1.
All inputs are finite; a program needn't handle non-finite values.
Results may differ from the reference program's by a relative error of at most 0.0028.
Values sent between devices are 32-bit elements; how exact they have to be, the bound alone decides.
A program may use at most 64 MiB of HBM per device.

```python
import jax
import jax.numpy as jnp
from jax import lax

NV = 128
NAUX = 256
NO = 32


def draw_pno_counts(key, part):
    key = jax.random.fold_in(key, 11)
    drawn = jax.random.randint(key, (NO, NO), NV // 4, NV + 1)
    row_ids = lax.broadcasted_iota(jnp.int32, (NO, NO), 0)
    col_ids = lax.broadcasted_iota(jnp.int32, (NO, NO), 1)
    symmetric = jnp.where(row_ids <= col_ids, drawn, drawn.T)
    symmetric = jnp.where(row_ids == col_ids, NV, symmetric)
    lowest_pair = (row_ids == 0) & (col_ids == 1) | (row_ids == 1) & (col_ids == 0)
    return jnp.where(lowest_pair, NV // 4, symmetric).astype(jnp.int32)


def draw_pair_live(key, part):
    key = jax.random.fold_in(key, 23)
    drawn = jax.random.randint(key, (NO, NO), 0, 4)
    row_ids = lax.broadcasted_iota(jnp.int32, (NO, NO), 0)
    col_ids = lax.broadcasted_iota(jnp.int32, (NO, NO), 1)
    symmetric = jnp.where(row_ids <= col_ids, drawn, drawn.T)
    flags = jnp.where(symmetric > 0, 1, 0)
    return jnp.where(row_ids == col_ids, 1, flags).astype(jnp.int32)


def levels(rng, dims, pieces, smallest, high):
    def one(axis_at, parts):
        draws = jax.random.uniform(jax.random.fold_in(jax.random.fold_in(rng, 6), axis_at), (parts,), jnp.float32, smallest / len(pieces), high / len(pieces))
        return jnp.repeat(jnp.exp(draws), dims[axis_at] // parts).reshape((-1,) + (1,) * (len(dims) - axis_at - 1))

    level = one(*pieces[0])
    for cut in pieces[1:]:
        level = level * one(*cut)
    return level


def centred(key, dims, scale, bound, split=(), kind=jnp.bfloat16):
    gain = levels(key, dims, split, -0.22, 0.18) if split else 1.0
    result = jax.random.normal(key, dims, jnp.float32) * scale * gain
    return jnp.minimum(jnp.maximum(result, -bound), bound).astype(kind)


def setup_inputs(seed: int = 0) -> dict:
    streams_of = jax.random.split(jax.random.key(seed), 5)
    return {
        "amplitudes": centred(streams_of[0], (NO, NO, NV, NV), 1.0, 6.0, ((0, 8), (1, 16))),
        "factors": centred(streams_of[1], (NO // 4, NO // 2, NAUX, NV, NV), (NV * max(NAUX // 16, 4)) ** -0.5, 0.125, ((0, 8), (1, 16), (2, 4))),
        "pno_counts": draw_pno_counts(jax.random.fold_in(streams_of[4], 71), 0),
        "pair_live": draw_pair_live(jax.random.fold_in(streams_of[4], 71), 0),
    }


def reference(amplitudes, factors, pno_counts, pair_live):
    positions = jnp.arange(NV, dtype=jnp.int32)
    inside = positions[None, None, :] < pno_counts[:, :, None]

    def one_pair(pair_index):
        row_occ = pair_index // NO
        col_occ = pair_index % NO
        domain = factors[row_occ // 4, col_occ // 2].astype(jnp.float32)
        weight_in = inside[row_occ, col_occ].astype(jnp.bfloat16)
        masked = amplitudes[row_occ, col_occ] * weight_in[:, None] * weight_in[None, :]
        half_tile = jnp.einsum("qac,cd->qad", domain, masked.astype(jnp.float32), precision=lax.Precision.HIGHEST).astype(jnp.bfloat16)
        return jnp.einsum("qad,qbd->ab", half_tile.astype(jnp.float32), domain, precision=lax.Precision.HIGHEST)

    ladder = lax.map(one_pair, jnp.arange(NO * NO, dtype=jnp.int32)).reshape(NO, NO, NV, NV)
    combined = ladder + jnp.transpose(ladder, (1, 0, 3, 2))
    kept_cells = inside[:, :, :, None] & inside[:, :, None, :] & (pair_live[:, :, None, None] > 0)
    return jnp.where(kept_cells, combined, jnp.zeros_like(combined))
```

```python
import jax
import jax.numpy as jnp
from jax import lax
from jax.experimental import pallas as pl
from jax.experimental.pallas import tpu as pltpu
from jax.sharding import PartitionSpec as P

MESH = pl.DeviceIdType.MESH
VIRT = 128
AUX = 64
SLAB = 32
QC = 32
LOADS = 4


def shift(row, bx, dy):
    return ((row // 4 + bx) % 2) * 4 + (row % 4 + dy) % 4


ROUTES = [(h, vd, vd % 2, 2 * (vd // 2) + h) for h in range(2) for vd in range(4)]


def kernel(
    amps,
    factors,
    counts,
    live,
    out,
    raw,
    fac,
    masked,
    acc,
    part,
    part_in,
    own,
    turned,
    relay,
    mirror,
    amp_sem,
    fac_sem,
    part_send,
    part_recv,
    relay_send,
    relay_recv,
    mirror_send,
    mirror_recv,
):
    R = lax.axis_index("row")
    z = lax.axis_index("col")
    v = lax.axis_index("vc")
    k = z % 2
    x_hi, core = v // 2, v % 2
    peers = {1: v + 1 - 2 * core, 2: (v + 2) % 4, 3: 3 - v}

    amp_copy = pltpu.make_async_copy(amps, raw, amp_sem)
    amp_copy.start()
    step_q = AUX // LOADS
    fac_copies = [
        pltpu.make_async_copy(
            factors.at[0, 0, pl.ds(n * step_q, step_q)],
            fac.at[pl.ds(n * step_q, step_q)],
            fac_sem.at[n],
        )
        for n in range(LOADS)
    ]
    for copy in fac_copies:
        copy.start()

    barrier = pltpu.get_barrier_semaphore()
    waits = 0
    for d in (1, 2, 3):
        pl.semaphore_signal(barrier, inc=1, device_id=(R, z, peers[d]), device_id_type=MESH)
        waits += 1
    for _, _, bx, dy in ROUTES:
        if bx or dy:
            pl.semaphore_signal(
                barrier, inc=1, device_id=(shift(R, bx, 4 - dy), z, v), device_id_type=MESH
            )
            waits += 1
    bx_in, dy_in = v % 2, 2 * (v // 2) + k
    row_in = shift(z // 2, bx_in, dy_in)
    for vs in range(4):
        for ks in range(2):
            not_here = jnp.logical_not((row_in == R) & (2 * R + ks == z) & (v == vs))

            @pl.when(not_here)
            def _():
                pl.semaphore_signal(
                    barrier, inc=1, device_id=(row_in, 2 * R + ks, vs), device_id_type=MESH
                )

            waits = waits + not_here.astype(jnp.int32)

    amp_copy.wait()
    rows = lax.broadcasted_iota(jnp.int32, (VIRT, VIRT), 0)
    cols = lax.broadcasted_iota(jnp.int32, (VIRT, VIRT), 1)
    reach = jnp.maximum(rows, cols)
    for s in range(4):
        for t in range(2):
            g, p = s // 2, (s % 2) * 2 + t
            tile = jnp.where(reach < counts[s, t], raw[s, t].astype(jnp.float32), 0.0)
            masked[g, :, p * VIRT : (p + 1) * VIRT] = tile.astype(jnp.bfloat16)
    for copy in fac_copies:
        copy.wait()

    def part_copy(g, d):
        src = part.at[g, 1, 1 - core] if d == 1 else part.at[g, 0, core if d == 2 else 1 - core]
        return pltpu.make_async_remote_copy(
            src_ref=src,
            dst_ref=part_in.at[g, d - 1],
            send_sem=part_send.at[g, d - 1],
            recv_sem=part_recv.at[g, d - 1],
            device_id=(R, z, peers[d]),
            device_id_type=MESH,
        )

    def relay_copy(h, vd, bx, dy):
        i = h * 4 + vd
        return pltpu.make_async_remote_copy(
            src_ref=turned.at[i],
            dst_ref=relay.at[i],
            send_sem=relay_send.at[i],
            recv_sem=relay_recv.at[i],
            device_id=(shift(R, bx, dy), z, v),
            device_id_type=MESH,
        )

    def last_leg(h, vd, bx, dy):
        i = h * 4 + vd
        row_from = shift(R, bx, 4 - dy)
        here = (z // 2 == R) & (2 * row_from + h == z) & (v == vd)
        src = relay if bx or dy else turned

        def remote():
            return pltpu.make_async_remote_copy(
                src_ref=src.at[i],
                dst_ref=mirror.at[v, k],
                send_sem=mirror_send.at[i],
                recv_sem=mirror_recv.at[v, k],
                device_id=(z // 2, 2 * row_from + h, vd),
                device_id_type=MESH,
            )

        def local():
            return pltpu.make_async_copy(src.at[i], mirror.at[v, k], mirror_recv.at[v, k])

        return here, remote, local

    def reduce_and_turn(g):
        for d in (1, 2, 3):
            part_copy(g, d).wait_recv()
        total = part[g, 1, core] + part_in[g, 0] + part_in[g, 1] + part_in[g, 2]
        own[g] = total
        flat = jnp.transpose(total)
        for vd in range(4):
            turned[g * 4 + vd] = flat[vd * SLAB : (vd + 1) * SLAB]
        for h, vd, bx, dy in ROUTES:
            if h == g and (bx or dy):
                relay_copy(h, vd, bx, dy).start()
        for h, vd, bx, dy in ROUTES:
            if h == g and not (bx or dy):
                start_last_leg(h, vd, bx, dy)

    def start_last_leg(h, vd, bx, dy):
        here, remote, local = last_leg(h, vd, bx, dy)

        @pl.when(here)
        def _():
            local().start()

        @pl.when(jnp.logical_not(here))
        def _():
            remote().start()

    def forward(g):
        for h, vd, bx, dy in ROUTES:
            if h == g and (bx or dy):
                relay_copy(h, vd, bx, dy).wait_recv()
                start_last_leg(h, vd, bx, dy)

    def body(j, carry):
        step, q0 = j // 2, (j % 2) * QC
        g, near = step // 2, step % 2
        half = x_hi * near + (1 - x_hi) * (1 - near)
        first_row = pl.multiple_of(half * 2 * SLAB, 2 * SLAB)
        domain = fac[pl.ds(q0, QC)]
        lhs = fac[pl.ds(q0, QC), pl.ds(first_row, 2 * SLAB), :].reshape(QC * 2 * SLAB, VIRT)
        mid = jnp.dot(lhs, masked[g], preferred_element_type=jnp.float32).astype(jnp.bfloat16)
        height = 2 * SLAB
        wide = jnp.concatenate(
            [
                jnp.concatenate(
                    [
                        mid[q * height : (q + 1) * height, p * VIRT : (p + 1) * VIRT]
                        for q in range(QC)
                    ],
                    axis=1,
                )
                for p in range(4)
            ],
            axis=0,
        )
        flat = jnp.concatenate([domain[q] for q in range(QC)], axis=1)
        term = lax.dot_general(
            wide, flat, (((1,), (1,)), ((), ())), preferred_element_type=jnp.float32
        )

        @pl.when(j % 2 == 0)
        def _():
            acc[...] = term

        @pl.when(j % 2 == 1)
        def _():
            total = acc[...] + term
            for c in range(2):
                for p in range(4):
                    at = p * height + c * SLAB
                    part[g, near, c, p * SLAB : (p + 1) * SLAB, :] = total[at : at + SLAB]

        return carry

    def with_sends(j, carry):
        body(j, carry)

        @pl.when(j == 5)
        def _():
            part_copy(1, 2).start()
            part_copy(1, 3).start()

        for gg in range(2):

            @pl.when(j == 4 * gg + 3)
            def _():
                part_copy(gg, 1).start()

        @pl.when(j == 4)
        def _():
            reduce_and_turn(0)

        @pl.when(j == 6)
        def _():
            forward(0)

        return carry

    lax.fori_loop(0, 2, body, 0)
    pl.semaphore_wait(barrier, waits)
    part_copy(0, 2).start()
    part_copy(0, 3).start()
    lax.fori_loop(2, 8, with_sends, 0)
    reduce_and_turn(1)
    forward(1)

    row_ids = v * SLAB + lax.broadcasted_iota(jnp.int32, (SLAB, VIRT), 0)
    col_ids = lax.broadcasted_iota(jnp.int32, (SLAB, VIRT), 1)
    reach_out = jnp.maximum(row_ids, col_ids)
    for ks in range(2):
        for vs in range(4):
            pltpu.make_async_copy(
                mirror.at[vs, ks], mirror.at[vs, ks], mirror_recv.at[vs, ks]
            ).wait()
        pieces = [mirror[vs, ks] for vs in range(4)]
        for sl in range(2):
            for t in range(2):
                p_own, p_in = sl * 2 + t, t * 2 + sl
                flipped = jnp.zeros((SLAB, VIRT), jnp.float32)
                for vs in range(4):
                    turn = ((vs - p_in) % 4) * SLAB
                    moved = pltpu.roll(pieces[vs], turn, 1) if turn else pieces[vs]
                    flipped = jnp.where(col_ids // SLAB == vs, moved, flipped)
                s = 2 * ks + sl
                summed = own[ks, p_own * SLAB : (p_own + 1) * SLAB, :] + flipped
                limit = jnp.where(live[s, t] > 0, counts[s, t], 0)
                out[s, t] = jnp.where(reach_out < limit, summed, 0.0)

    for g in range(2):
        for d in (1, 2, 3):
            part_copy(g, d).wait_send()
    for h, vd, bx, dy in ROUTES:
        if bx or dy:
            relay_copy(h, vd, bx, dy).wait_send()
        here, remote, _ = last_leg(h, vd, bx, dy)

        @pl.when(jnp.logical_not(here))
        def _():
            remote().wait_send()


def on_device(amplitudes, factors, pno_counts, pair_live):
    dma = pltpu.SemaphoreType.DMA
    tile = (4 * SLAB, VIRT)
    return pl.pallas_call(
        kernel,
        out_shape=jax.ShapeDtypeStruct((4, 2, SLAB, VIRT), jnp.float32),
        in_specs=[
            pl.BlockSpec(memory_space=pl.ANY),
            pl.BlockSpec(memory_space=pl.ANY),
            pl.BlockSpec(memory_space=pltpu.SMEM),
            pl.BlockSpec(memory_space=pltpu.SMEM),
        ],
        out_specs=pl.BlockSpec(memory_space=pltpu.VMEM),
        scratch_shapes=[
            pltpu.VMEM((4, 2, VIRT, VIRT), jnp.bfloat16),
            pltpu.VMEM((AUX, VIRT, VIRT), jnp.bfloat16),
            pltpu.VMEM((2, VIRT, 4 * VIRT), jnp.bfloat16),
            pltpu.VMEM((8 * SLAB, VIRT), jnp.float32),
            pltpu.VMEM((2, 2, 2) + tile, jnp.float32),
            pltpu.VMEM((2, 3) + tile, jnp.float32),
            pltpu.VMEM((2,) + tile, jnp.float32),
            pltpu.VMEM((8, SLAB, VIRT), jnp.float32),
            pltpu.VMEM((8, SLAB, VIRT), jnp.float32),
            pltpu.VMEM((4, 2, SLAB, VIRT), jnp.float32),
            dma,
            dma((LOADS,)),
            dma((2, 3)),
            dma((2, 3)),
            dma((8,)),
            dma((8,)),
            dma((8,)),
            dma((4, 2)),
        ],
        compiler_params=pltpu.CompilerParams(
            collective_id=0, has_side_effects=True, vmem_limit_bytes=48 << 20
        ),
        name="ladder",
    )(amplitudes, factors, pno_counts, pair_live)


def solution(mesh):
    in_specs = (
        P("row", "col", None, None),
        P("row", "col", "vc", None, None),
        P("row", "col"),
        P("row", "col"),
    )
    out_specs = P("row", "col", "vc", None)
    return jax.shard_map(
        on_device, mesh=mesh, in_specs=in_specs, out_specs=out_specs, check_vma=False
    )
```

```python
import jax
import jax.numpy as jnp
from jax import lax
from jax.experimental import pallas as pl
from jax.experimental.pallas import tpu as pltpu
from jax.sharding import PartitionSpec as P

MESH = pl.DeviceIdType.MESH
VIRT = 128
AUX = 64
SLAB = 32
QC = 32
LOADS = 4


def shift(row, bx, dy):
    return ((row // 4 + bx) % 2) * 4 + (row % 4 + dy) % 4


def route(h, vd):
    return vd % 2, vd // 2


ROUTES = [(h, vd) + route(h, vd) for h in range(2) for vd in range(4)]


def kernel(
    amps,
    factors,
    counts_in,
    live_in,
    out,
    counts,
    live,
    raw,
    fac,
    masked,
    acc,
    part,
    part_in,
    own,
    turned,
    relay,
    mirror,
    small_sem,
    amp_sem,
    fac_sem,
    part_send,
    part_recv,
    relay_send,
    relay_recv,
    mirror_send,
    mirror_recv,
):
    R = lax.axis_index("row")
    z = lax.axis_index("col")
    v = lax.axis_index("vc")
    k = z % 2
    x_hi, core = v // 2, v % 2
    peers = {1: v + 1 - 2 * core, 2: (v + 2) % 4, 3: 3 - v}

    amp_copy = pltpu.make_async_copy(amps, raw, amp_sem)
    amp_copy.start()
    small_copies = [
        pltpu.make_async_copy(counts_in, counts, small_sem.at[0]),
        pltpu.make_async_copy(live_in, live, small_sem.at[1]),
    ]
    for copy in small_copies:
        copy.start()
    step_q = AUX // LOADS
    fac_copies = [
        pltpu.make_async_copy(
            factors.at[0, 0, pl.ds(n * step_q, step_q)],
            fac.at[pl.ds(n * step_q, step_q)],
            fac_sem.at[n],
        )
        for n in range(LOADS)
    ]
    for copy in fac_copies:
        copy.start()

    barrier = pltpu.get_barrier_semaphore()
    waits = 0
    for d in (1, 2, 3):
        pl.semaphore_signal(barrier, inc=1, device_id=(R, z, peers[d]), device_id_type=MESH)
        waits += 1
    for _, _, bx, dy in ROUTES:
        if bx or dy:
            pl.semaphore_signal(
                barrier, inc=1, device_id=(shift(R, bx, 4 - dy), z, v), device_id_type=MESH
            )
            waits += 1
    bx_in, dy_in = route(k, v)
    row_in = shift(z // 2, bx_in, dy_in)
    for vs in range(4):
        for ks in range(2):
            not_here = jnp.logical_not((row_in == R) & (2 * R + ks == z) & (v == vs))

            @pl.when(not_here)
            def _():
                pl.semaphore_signal(
                    barrier, inc=1, device_id=(row_in, 2 * R + ks, vs), device_id_type=MESH
                )

            waits = waits + not_here.astype(jnp.int32)

    for copy in small_copies:
        copy.wait()
    amp_copy.wait()
    rows = lax.broadcasted_iota(jnp.int32, (VIRT, VIRT), 0)
    cols = lax.broadcasted_iota(jnp.int32, (VIRT, VIRT), 1)
    reach = jnp.maximum(rows, cols)
    for s in range(4):
        for t in range(2):
            g, p = s // 2, (s % 2) * 2 + t
            tile = jnp.where(reach < counts[t, s], raw[s, t].astype(jnp.float32), 0.0)
            masked[g, :, p * VIRT : (p + 1) * VIRT] = tile.astype(jnp.bfloat16)

    def part_copy(g, d):
        src = part.at[g, 1, 1 - core] if d == 1 else part.at[g, 0, core if d == 2 else 1 - core]
        return pltpu.make_async_remote_copy(
            src_ref=src,
            dst_ref=part_in.at[g, d - 1],
            send_sem=part_send.at[g, d - 1],
            recv_sem=part_recv.at[g, d - 1],
            device_id=(R, z, peers[d]),
            device_id_type=MESH,
        )

    def relay_copy(h, vd, bx, dy):
        i = h * 4 + vd
        return pltpu.make_async_remote_copy(
            src_ref=turned.at[i],
            dst_ref=relay.at[i],
            send_sem=relay_send.at[i],
            recv_sem=relay_recv.at[i],
            device_id=(shift(R, bx, dy), z, v),
            device_id_type=MESH,
        )

    def last_leg(h, vd, bx, dy):
        i = h * 4 + vd
        row_from = shift(R, bx, 4 - dy)
        here = (z // 2 == R) & (2 * row_from + h == z) & (v == vd)
        src = relay if bx or dy else turned

        def remote():
            return pltpu.make_async_remote_copy(
                src_ref=src.at[i],
                dst_ref=mirror.at[v, k],
                send_sem=mirror_send.at[i],
                recv_sem=mirror_recv.at[v, k],
                device_id=(z // 2, 2 * row_from + h, vd),
                device_id_type=MESH,
            )

        def local():
            return pltpu.make_async_copy(src.at[i], mirror.at[v, k], mirror_recv.at[v, k])

        return here, remote, local

    def reduce_and_turn(g):
        for d in (1, 2, 3):
            part_copy(g, d).wait_recv()
        total = part[g, 1, core] + part_in[g, 0] + part_in[g, 1] + part_in[g, 2]
        own[g] = total
        flat = jnp.transpose(total)
        for vd in range(4):
            turned[g * 4 + vd] = flat[vd * SLAB : (vd + 1) * SLAB]
        for h, vd, bx, dy in ROUTES:
            if h == g and (bx or dy):
                relay_copy(h, vd, bx, dy).start()
        for h, vd, bx, dy in ROUTES:
            if h == g and not (bx or dy):
                start_last_leg(h, vd, bx, dy)

    def start_last_leg(h, vd, bx, dy):
        here, remote, local = last_leg(h, vd, bx, dy)

        @pl.when(here)
        def _():
            local().start()

        @pl.when(jnp.logical_not(here))
        def _():
            remote().start()

    def forward(g):
        for h, vd, bx, dy in ROUTES:
            if h == g and (bx or dy):
                relay_copy(h, vd, bx, dy).wait_recv()
                start_last_leg(h, vd, bx, dy)

    def products(g, first_row, height, q0):
        domain = fac[pl.ds(q0, QC)]
        lhs = fac[pl.ds(q0, QC), pl.ds(first_row, height), :].reshape(QC * height, VIRT)
        mid = jnp.dot(lhs, masked[g], preferred_element_type=jnp.float32).astype(jnp.bfloat16)
        wide = jnp.concatenate(
            [
                jnp.concatenate(
                    [
                        mid[q * height : (q + 1) * height, p * VIRT : (p + 1) * VIRT]
                        for q in range(QC)
                    ],
                    axis=1,
                )
                for p in range(4)
            ],
            axis=0,
        )
        flat = jnp.concatenate([domain[q] for q in range(QC)], axis=1)
        return lax.dot_general(
            wide, flat, (((1,), (1,)), ((), ())), preferred_element_type=jnp.float32
        )

    far_row = pl.multiple_of((1 - x_hi) * 2 * SLAB, 2 * SLAB)
    near_row = pl.multiple_of(x_hi * 2 * SLAB, 2 * SLAB)

    def store_parts(g, near, total):
        for c in range(2):
            for p in range(4):
                at = (2 * p + c) * SLAB
                part[g, near, c, p * SLAB : (p + 1) * SLAB, :] = total[at : at + SLAB]

    def all_products(g, first_row, height):
        return lax.fori_loop(
            0,
            AUX // QC,
            lambda n, total: total + products(g, first_row, height, n * QC),
            jnp.zeros((4 * height, VIRT), jnp.float32),
        )

    for copy in fac_copies[: LOADS // 2]:
        copy.wait()
    acc[...] = products(0, far_row, 2 * SLAB, 0)
    for copy in fac_copies[LOADS // 2 :]:
        copy.wait()
    store_parts(0, 0, acc[...] + products(0, far_row, 2 * SLAB, QC))
    pl.semaphore_wait(barrier, waits)
    part_copy(0, 2).start()
    part_copy(0, 3).start()
    store_parts(1, 0, all_products(1, far_row, 2 * SLAB))
    part_copy(1, 2).start()
    part_copy(1, 3).start()
    store_parts(0, 1, all_products(0, near_row, 2 * SLAB))
    part_copy(0, 1).start()
    peer_row = pl.multiple_of(near_row + (1 - core) * SLAB, SLAB)
    part[1, 1, 1 - core] = all_products(1, peer_row, SLAB)
    part_copy(1, 1).start()
    reduce_and_turn(0)
    own_row = pl.multiple_of(near_row + core * SLAB, SLAB)
    part[1, 1, core] = all_products(1, own_row, SLAB)
    reduce_and_turn(1)
    forward(0)
    forward(1)

    row_ids = v * SLAB + lax.broadcasted_iota(jnp.int32, (SLAB, VIRT), 0)
    col_ids = lax.broadcasted_iota(jnp.int32, (SLAB, VIRT), 1)
    reach_out = jnp.maximum(row_ids, col_ids)
    for ks in range(2):
        for vs in range(4):
            pltpu.make_async_copy(
                mirror.at[vs, ks], mirror.at[vs, ks], mirror_recv.at[vs, ks]
            ).wait()
        pieces = [mirror[vs, ks] for vs in range(4)]
        for sl in range(2):
            for t in range(2):
                p_own, p_in = sl * 2 + t, t * 2 + sl
                flipped = jnp.zeros((SLAB, VIRT), jnp.float32)
                for vs in range(4):
                    turn = ((vs - p_in) % 4) * SLAB
                    moved = pltpu.roll(pieces[vs], turn, 1) if turn else pieces[vs]
                    flipped = jnp.where(col_ids // SLAB == vs, moved, flipped)
                s = 2 * ks + sl
                summed = own[ks, p_own * SLAB : (p_own + 1) * SLAB, :] + flipped
                limit = jnp.where(live[t, s] > 0, counts[t, s], 0)
                out[s, t] = jnp.where(reach_out < limit, summed, 0.0)

    for g in range(2):
        for d in (1, 2, 3):
            part_copy(g, d).wait_send()
    for h, vd, bx, dy in ROUTES:
        if bx or dy:
            relay_copy(h, vd, bx, dy).wait_send()
        here, remote, _ = last_leg(h, vd, bx, dy)

        @pl.when(jnp.logical_not(here))
        def _():
            remote().wait_send()


def on_device(amplitudes, factors, pno_counts, pair_live):
    arguments = (amplitudes, factors, pno_counts.T, pair_live.T)
    dma = pltpu.SemaphoreType.DMA
    tile = (4 * SLAB, VIRT)
    return pl.pallas_call(
        kernel,
        out_shape=jax.ShapeDtypeStruct((4, 2, SLAB, VIRT), jnp.float32),
        in_specs=[pl.BlockSpec(memory_space=pltpu.HBM)] * 4,
        out_specs=pl.BlockSpec(memory_space=pltpu.VMEM),
        scratch_shapes=[
            pltpu.SMEM((2, 4), jnp.int32),
            pltpu.SMEM((2, 4), jnp.int32),
            pltpu.VMEM((4, 2, VIRT, VIRT), jnp.bfloat16),
            pltpu.VMEM((AUX, VIRT, VIRT), jnp.bfloat16),
            pltpu.VMEM((2, VIRT, 4 * VIRT), jnp.bfloat16),
            pltpu.VMEM((8 * SLAB, VIRT), jnp.float32),
            pltpu.VMEM((2, 2, 2) + tile, jnp.float32),
            pltpu.VMEM((2, 3) + tile, jnp.float32),
            pltpu.VMEM((2,) + tile, jnp.float32),
            pltpu.VMEM((8, SLAB, VIRT), jnp.float32),
            pltpu.VMEM((8, SLAB, VIRT), jnp.float32),
            pltpu.VMEM((4, 2, SLAB, VIRT), jnp.float32),
            dma((2,)),
            dma,
            dma((LOADS,)),
            dma((2, 3)),
            dma((2, 3)),
            dma((8,)),
            dma((8,)),
            dma((8,)),
            dma((4, 2)),
        ],
        compiler_params=pltpu.CompilerParams(
            collective_id=0, has_side_effects=True, vmem_limit_bytes=48 << 20
        ),
        name="ladder",
    )(*(pltpu.with_memory_space_constraint(a, pltpu.HBM) for a in arguments))


def solution(mesh):
    in_specs = (
        P("row", "col", None, None),
        P("row", "col", "vc", None, None),
        P("row", "col"),
        P("row", "col"),
    )
    out_specs = P("row", "col", "vc", None)
    return jax.shard_map(
        on_device, mesh=mesh, in_specs=in_specs, out_specs=out_specs, check_vma=False
    )
```

```python
import jax
import jax.numpy as jnp
from jax import lax
from jax.experimental import pallas as pl
from jax.experimental.pallas import tpu as pltpu
from jax.sharding import PartitionSpec as P

MESH = pl.DeviceIdType.MESH
VIRT = 128
AUX = 64
SLAB = 32
QC = 4
MEETS = (2, 3, 1, 0)
LOADS = 4


def shift(row, bx, dy):
    return ((row // 4 + bx) % 2) * 4 + (row % 4 + dy) % 4


def route(h, vd):
    return vd % 2, vd // 2


ROUTES = [(h, vd) + route(h, vd) for h in range(2) for vd in range(4)]


def kernel(
    amps,
    factors,
    counts_in,
    live_in,
    out,
    counts,
    live,
    raw,
    fac,
    masked,
    part,
    part_in,
    own,
    turned,
    relay,
    mirror,
    small_sem,
    amp_sem,
    fac_sem,
    part_send,
    part_recv,
    relay_send,
    relay_recv,
    mirror_send,
    mirror_recv,
):
    R = lax.axis_index("row")
    z = lax.axis_index("col")
    v = lax.axis_index("vc")
    k = z % 2
    x_hi, core = v // 2, v % 2
    peers = {1: v + 1 - 2 * core, 2: (v + 2) % 4, 3: 3 - v}

    amp_copy = pltpu.make_async_copy(amps, raw, amp_sem)
    amp_copy.start()
    small_copies = [
        pltpu.make_async_copy(counts_in, counts, small_sem.at[0]),
        pltpu.make_async_copy(live_in, live, small_sem.at[1]),
    ]
    for copy in small_copies:
        copy.start()
    step_q = AUX // LOADS
    fac_copies = [
        pltpu.make_async_copy(
            factors.at[0, 0, pl.ds(n * step_q, step_q)],
            fac.at[pl.ds(n * step_q, step_q)],
            fac_sem.at[n],
        )
        for n in range(LOADS)
    ]
    for copy in fac_copies:
        copy.start()

    barrier = pltpu.get_barrier_semaphore()
    waits = 0
    for d in (1, 2, 3):
        pl.semaphore_signal(barrier, inc=1, device_id=(R, z, peers[d]), device_id_type=MESH)
        waits += 1
    for _, _, bx, dy in ROUTES:
        if bx or dy:
            pl.semaphore_signal(
                barrier, inc=1, device_id=(shift(R, bx, 4 - dy), z, v), device_id_type=MESH
            )
            waits += 1
    bx_in, dy_in = route(k, v)
    row_in = shift(z // 2, bx_in, dy_in)
    for vs in range(4):
        for ks in range(2):
            not_here = jnp.logical_not((row_in == R) & (2 * R + ks == z) & (v == vs))

            @pl.when(not_here)
            def _():
                pl.semaphore_signal(
                    barrier, inc=1, device_id=(row_in, 2 * R + ks, vs), device_id_type=MESH
                )

            waits = waits + not_here.astype(jnp.int32)

    for copy in small_copies:
        copy.wait()
    amp_copy.wait()
    rows = lax.broadcasted_iota(jnp.int32, (VIRT, VIRT), 0)
    cols = lax.broadcasted_iota(jnp.int32, (VIRT, VIRT), 1)
    reach = jnp.maximum(rows, cols)
    for s in range(4):
        for t in range(2):
            g, p = s // 2, (s % 2) * 2 + t
            tile = jnp.where(reach < counts[t, s], raw[s, t].astype(jnp.float32), 0.0)
            masked[g, :, p * VIRT : (p + 1) * VIRT] = tile.astype(jnp.bfloat16)

    def part_copy(g, d):
        src = part.at[g, 1, 1 - core] if d == 1 else part.at[g, 0, core if d == 2 else 1 - core]
        return pltpu.make_async_remote_copy(
            src_ref=src,
            dst_ref=part_in.at[g, d - 1],
            send_sem=part_send.at[g, d - 1],
            recv_sem=part_recv.at[g, d - 1],
            device_id=(R, z, peers[d]),
            device_id_type=MESH,
        )

    def relay_copy(h, vd, bx, dy):
        i = h * 4 + vd
        return pltpu.make_async_remote_copy(
            src_ref=turned.at[i],
            dst_ref=relay.at[i],
            send_sem=relay_send.at[i],
            recv_sem=relay_recv.at[i],
            device_id=(shift(R, bx, dy), z, v),
            device_id_type=MESH,
        )

    def last_leg(h, vd, bx, dy):
        i = h * 4 + vd
        row_from = shift(R, bx, 4 - dy)
        here = (z // 2 == R) & (2 * row_from + h == z) & (v == vd)
        src = relay if bx or dy else turned

        def remote():
            return pltpu.make_async_remote_copy(
                src_ref=src.at[i],
                dst_ref=mirror.at[v, k],
                send_sem=mirror_send.at[i],
                recv_sem=mirror_recv.at[v, k],
                device_id=(z // 2, 2 * row_from + h, vd),
                device_id_type=MESH,
            )

        def local():
            return pltpu.make_async_copy(src.at[i], mirror.at[v, k], mirror_recv.at[v, k])

        return here, remote, local

    def reduce_and_turn(g):
        for d in (1, 2, 3):
            part_copy(g, d).wait_recv()
        total = part[g, 1, core] + part_in[g, 0] + part_in[g, 1] + part_in[g, 2]
        own[g] = total
        flat = jnp.transpose(total)
        for vd in range(4):
            turned[g * 4 + vd] = flat[vd * SLAB : (vd + 1) * SLAB]
        for h, vd, bx, dy in ROUTES:
            if h == g and (bx or dy):
                relay_copy(h, vd, bx, dy).start()
        for h, vd, bx, dy in ROUTES:
            if h == g and not (bx or dy):
                start_last_leg(h, vd, bx, dy)

    def start_last_leg(h, vd, bx, dy):
        here, remote, local = last_leg(h, vd, bx, dy)

        @pl.when(here)
        def _():
            local().start()

        @pl.when(jnp.logical_not(here))
        def _():
            remote().start()

    def forward(g):
        for h, vd, bx, dy in ROUTES:
            if h == g and (bx or dy):
                relay_copy(h, vd, bx, dy).wait_recv()
                start_last_leg(h, vd, bx, dy)

    def products(g, first_row, height, q0):
        domain = fac[pl.ds(q0, QC)]
        lhs = fac[pl.ds(q0, QC), pl.ds(first_row, height), :].reshape(QC * height, VIRT)
        mid = jnp.dot(lhs, masked[g], preferred_element_type=jnp.float32).astype(jnp.bfloat16)
        wide = jnp.concatenate(
            [
                jnp.concatenate(
                    [
                        mid[q * height : (q + 1) * height, p * VIRT : (p + 1) * VIRT]
                        for q in range(QC)
                    ],
                    axis=1,
                )
                for p in range(4)
            ],
            axis=0,
        )
        flat = jnp.concatenate([domain[q] for q in range(QC)], axis=1)
        return lax.dot_general(
            wide, flat, (((1,), (1,)), ((), ())), preferred_element_type=jnp.float32
        )

    far_row = pl.multiple_of((1 - x_hi) * 2 * SLAB, 2 * SLAB)
    near_row = pl.multiple_of(x_hi * 2 * SLAB, 2 * SLAB)

    def store_parts(g, near, total):
        for c in range(2):
            for p in range(4):
                at = (2 * p + c) * SLAB
                part[g, near, c, p * SLAB : (p + 1) * SLAB, :] = total[at : at + SLAB]

    def sum_products(g, first_row, height, start, stop):
        total = products(g, first_row, height, start)
        for q0 in range(start + QC, stop, QC):
            total = total + products(g, first_row, height, q0)
        return total

    fresh = (((0, 2), (0, 3)), ((1, 2), (1, 3)), ((0, 1),), ((1, 1),))

    def send_parts(step):
        @pl.when(z // 4 == MEETS[step])
        def _():
            pl.semaphore_wait(barrier, waits)
            for group in fresh[: step + 1]:
                for g, d in group:
                    part_copy(g, d).start()

        for quarter in MEETS[:step]:

            @pl.when(z // 4 == quarter)
            def _():
                for g, d in fresh[step]:
                    part_copy(g, d).start()

    for copy in fac_copies:
        copy.wait()
    store_parts(0, 0, sum_products(0, far_row, 2 * SLAB, 0, AUX))
    send_parts(0)
    store_parts(1, 0, sum_products(1, far_row, 2 * SLAB, 0, AUX))
    send_parts(1)
    peer_row = pl.multiple_of(near_row + (1 - core) * SLAB, SLAB)
    own_row = pl.multiple_of(near_row + core * SLAB, SLAB)
    part[0, 1, 1 - core] = sum_products(0, peer_row, SLAB, 0, AUX)
    send_parts(2)
    part[0, 1, core] = sum_products(0, own_row, SLAB, 0, AUX)

    @pl.when(z // 4 == MEETS[0])
    def _():
        reduce_and_turn(0)

    part[1, 1, 1 - core] = sum_products(1, peer_row, SLAB, 0, AUX)
    send_parts(3)
    part[1, 1, core] = sum_products(1, own_row, SLAB, 0, AUX)

    @pl.when(z // 4 != MEETS[0])
    def _():
        reduce_and_turn(0)

    reduce_and_turn(1)
    forward(0)
    forward(1)

    row_ids = v * SLAB + lax.broadcasted_iota(jnp.int32, (SLAB, VIRT), 0)
    col_ids = lax.broadcasted_iota(jnp.int32, (SLAB, VIRT), 1)
    reach_out = jnp.maximum(row_ids, col_ids)
    for ks in range(2):
        for vs in range(4):
            pltpu.make_async_copy(
                mirror.at[vs, ks], mirror.at[vs, ks], mirror_recv.at[vs, ks]
            ).wait()
        pieces = [mirror[vs, ks] for vs in range(4)]
        for sl in range(2):
            for t in range(2):
                p_own, p_in = sl * 2 + t, t * 2 + sl
                flipped = jnp.zeros((SLAB, VIRT), jnp.float32)
                for vs in range(4):
                    turn = ((vs - p_in) % 4) * SLAB
                    moved = pltpu.roll(pieces[vs], turn, 1) if turn else pieces[vs]
                    flipped = jnp.where(col_ids // SLAB == vs, moved, flipped)
                s = 2 * ks + sl
                summed = own[ks, p_own * SLAB : (p_own + 1) * SLAB, :] + flipped
                limit = jnp.where(live[t, s] > 0, counts[t, s], 0)
                out[s, t] = jnp.where(reach_out < limit, summed, 0.0)

    for g in range(2):
        for d in (1, 2, 3):
            part_copy(g, d).wait_send()
    for h, vd, bx, dy in ROUTES:
        if bx or dy:
            relay_copy(h, vd, bx, dy).wait_send()
        here, remote, _ = last_leg(h, vd, bx, dy)

        @pl.when(jnp.logical_not(here))
        def _():
            remote().wait_send()


def on_device(amplitudes, factors, pno_counts, pair_live):
    arguments = (amplitudes, factors, pno_counts.T, pair_live.T)
    dma = pltpu.SemaphoreType.DMA
    tile = (4 * SLAB, VIRT)
    return pl.pallas_call(
        kernel,
        out_shape=jax.ShapeDtypeStruct((4, 2, SLAB, VIRT), jnp.float32),
        in_specs=[pl.BlockSpec(memory_space=pltpu.HBM)] * 4,
        out_specs=pl.BlockSpec(memory_space=pltpu.VMEM),
        scratch_shapes=[
            pltpu.SMEM((2, 4), jnp.int32),
            pltpu.SMEM((2, 4), jnp.int32),
            pltpu.VMEM((4, 2, VIRT, VIRT), jnp.bfloat16),
            pltpu.VMEM((AUX, VIRT, VIRT), jnp.bfloat16),
            pltpu.VMEM((2, VIRT, 4 * VIRT), jnp.bfloat16),
            pltpu.VMEM((2, 2, 2) + tile, jnp.float32),
            pltpu.VMEM((2, 3) + tile, jnp.float32),
            pltpu.VMEM((2,) + tile, jnp.float32),
            pltpu.VMEM((8, SLAB, VIRT), jnp.float32),
            pltpu.VMEM((8, SLAB, VIRT), jnp.float32),
            pltpu.VMEM((4, 2, SLAB, VIRT), jnp.float32),
            dma((2,)),
            dma,
            dma((LOADS,)),
            dma((2, 3)),
            dma((2, 3)),
            dma((8,)),
            dma((8,)),
            dma((8,)),
            dma((4, 2)),
        ],
        compiler_params=pltpu.CompilerParams(
            collective_id=0, has_side_effects=True, vmem_limit_bytes=48 << 20
        ),
        name="ladder",
    )(*(pltpu.with_memory_space_constraint(a, pltpu.HBM) for a in arguments))


def solution(mesh):
    in_specs = (
        P("row", "col", None, None),
        P("row", "col", "vc", None, None),
        P("row", "col"),
        P("row", "col"),
    )
    out_specs = P("row", "col", "vc", None)
    return jax.shard_map(
        on_device, mesh=mesh, in_specs=in_specs, out_specs=out_specs, check_vma=False
    )
```

```python
import jax
import jax.numpy as jnp
from jax import lax
from jax.experimental import pallas as pl
from jax.experimental.pallas import tpu as pltpu
from jax.sharding import PartitionSpec as P

MESH = pl.DeviceIdType.MESH
VIRT = 128
AUX = 64
SLAB = 32
QC = 4
MEETS = (2, 3, 1, 0)
LOADS = 4


def shift(row, bx, dy):
    return ((row // 4 + bx) % 2) * 4 + (row % 4 + dy) % 4


def route(h, vd):
    return vd % 2, vd // 2


ROUTES = [(h, vd) + route(h, vd) for h in range(2) for vd in range(4)]


def kernel(
    amps,
    factors,
    counts_in,
    live_in,
    out,
    counts,
    live,
    raw,
    fac,
    masked,
    part,
    part_in,
    own,
    turned,
    relay,
    mirror,
    small_sem,
    amp_sem,
    fac_sem,
    part_send,
    part_recv,
    relay_send,
    relay_recv,
    mirror_send,
    mirror_recv,
):
    R = lax.axis_index("row")
    z = lax.axis_index("col")
    v = lax.axis_index("vc")
    k = z % 2
    x_hi, core = v // 2, v % 2
    peers = {1: v + 1 - 2 * core, 2: (v + 2) % 4, 3: 3 - v}

    amp_copy = pltpu.make_async_copy(amps, raw, amp_sem)
    amp_copy.start()
    small_copies = [
        pltpu.make_async_copy(counts_in, counts, small_sem.at[0]),
        pltpu.make_async_copy(live_in, live, small_sem.at[1]),
    ]
    for copy in small_copies:
        copy.start()
    step_q = AUX // LOADS
    fac_copies = [
        pltpu.make_async_copy(
            factors.at[0, 0, pl.ds(n * step_q, step_q)],
            fac.at[pl.ds(n * step_q, step_q)],
            fac_sem.at[n],
        )
        for n in range(LOADS)
    ]
    for copy in fac_copies:
        copy.start()

    barrier = pltpu.get_barrier_semaphore()
    waits = 0
    for d in (1, 2, 3):
        pl.semaphore_signal(barrier, inc=1, device_id=(R, z, peers[d]), device_id_type=MESH)
        waits += 1
    for _, _, bx, dy in ROUTES:
        if bx or dy:
            pl.semaphore_signal(
                barrier, inc=1, device_id=(shift(R, bx, 4 - dy), z, v), device_id_type=MESH
            )
            waits += 1
    bx_in, dy_in = route(k, v)
    row_in = shift(z // 2, bx_in, dy_in)
    for vs in range(4):
        for ks in range(2):
            not_here = jnp.logical_not((row_in == R) & (2 * R + ks == z) & (v == vs))

            @pl.when(not_here)
            def _():
                pl.semaphore_signal(
                    barrier, inc=1, device_id=(row_in, 2 * R + ks, vs), device_id_type=MESH
                )

            waits = waits + not_here.astype(jnp.int32)

    for copy in small_copies:
        copy.wait()
    amp_copy.wait()
    rows = lax.broadcasted_iota(jnp.int32, (VIRT, VIRT), 0)
    cols = lax.broadcasted_iota(jnp.int32, (VIRT, VIRT), 1)
    reach = jnp.maximum(rows, cols)
    def mask_group(g):
        for sl in range(2):
            for t in range(2):
                s, p = 2 * g + sl, 2 * sl + t
                tile = jnp.where(reach < counts[t, s], raw[s, t].astype(jnp.float32), 0.0)
                masked[g, :, p * VIRT : (p + 1) * VIRT] = tile.astype(jnp.bfloat16)

    mask_group(0)

    def part_copy(g, d):
        src = part.at[g, 1, 1 - core] if d == 1 else part.at[g, 0, core if d == 2 else 1 - core]
        return pltpu.make_async_remote_copy(
            src_ref=src,
            dst_ref=part_in.at[g, d - 1],
            send_sem=part_send.at[g, d - 1],
            recv_sem=part_recv.at[g, d - 1],
            device_id=(R, z, peers[d]),
            device_id_type=MESH,
        )

    def relay_copy(h, vd, bx, dy):
        i = h * 4 + vd
        return pltpu.make_async_remote_copy(
            src_ref=turned.at[i],
            dst_ref=relay.at[i],
            send_sem=relay_send.at[i],
            recv_sem=relay_recv.at[i],
            device_id=(shift(R, bx, dy), z, v),
            device_id_type=MESH,
        )

    def last_leg(h, vd, bx, dy):
        i = h * 4 + vd
        row_from = shift(R, bx, 4 - dy)
        here = (z // 2 == R) & (2 * row_from + h == z) & (v == vd)
        src = relay if bx or dy else turned

        def remote():
            return pltpu.make_async_remote_copy(
                src_ref=src.at[i],
                dst_ref=mirror.at[v, k],
                send_sem=mirror_send.at[i],
                recv_sem=mirror_recv.at[v, k],
                device_id=(z // 2, 2 * row_from + h, vd),
                device_id_type=MESH,
            )

        def local():
            return pltpu.make_async_copy(src.at[i], mirror.at[v, k], mirror_recv.at[v, k])

        return here, remote, local

    def reduce_and_turn(g):
        for d in (1, 2, 3):
            part_copy(g, d).wait_recv()
        total = part[g, 1, core] + part_in[g, 0] + part_in[g, 1] + part_in[g, 2]
        own[g] = total
        flat = jnp.transpose(total)
        for vd in range(4):
            turned[g * 4 + vd] = flat[vd * SLAB : (vd + 1) * SLAB]
            if any(route(g, vd)):
                relay_copy(g, vd, *route(g, vd)).start()
        for h, vd, bx, dy in ROUTES:
            if h == g and not (bx or dy):
                start_last_leg(h, vd, bx, dy)

    def start_last_leg(h, vd, bx, dy):
        here, remote, local = last_leg(h, vd, bx, dy)

        @pl.when(here)
        def _():
            local().start()

        @pl.when(jnp.logical_not(here))
        def _():
            remote().start()

    def forward(g):
        for h, vd, bx, dy in ROUTES:
            if h == g and (bx or dy):
                relay_copy(h, vd, bx, dy).wait_recv()
                start_last_leg(h, vd, bx, dy)

    def products(g, first_row, height, q0):
        domain = fac[pl.ds(q0, QC)]
        lhs = fac[pl.ds(q0, QC), pl.ds(first_row, height), :].reshape(QC * height, VIRT)
        mid = jnp.dot(lhs, masked[g], preferred_element_type=jnp.float32).astype(jnp.bfloat16)
        wide = jnp.concatenate(
            [
                jnp.concatenate(
                    [
                        mid[q * height : (q + 1) * height, p * VIRT : (p + 1) * VIRT]
                        for q in range(QC)
                    ],
                    axis=1,
                )
                for p in range(4)
            ],
            axis=0,
        )
        flat = jnp.concatenate([domain[q] for q in range(QC)], axis=1)
        return lax.dot_general(
            wide, flat, (((1,), (1,)), ((), ())), preferred_element_type=jnp.float32
        )

    far_row = pl.multiple_of((1 - x_hi) * 2 * SLAB, 2 * SLAB)
    near_row = pl.multiple_of(x_hi * 2 * SLAB, 2 * SLAB)

    def store_parts(g, near, total):
        for c in range(2):
            for p in range(4):
                at = (2 * p + c) * SLAB
                part[g, near, c, p * SLAB : (p + 1) * SLAB, :] = total[at : at + SLAB]

    def sum_products(g, first_row, height, start, stop):
        total = products(g, first_row, height, start)
        for q0 in range(start + QC, stop, QC):
            total = total + products(g, first_row, height, q0)
        return total

    fresh = (((0, 2), (0, 3)), ((1, 2), (1, 3)), ((0, 1),), ((1, 1),))

    def send_parts(step):
        @pl.when(z // 4 == MEETS[step])
        def _():
            pl.semaphore_wait(barrier, waits)
            for group in fresh[: step + 1]:
                for g, d in group:
                    part_copy(g, d).start()

        for quarter in MEETS[:step]:

            @pl.when(z // 4 == quarter)
            def _():
                for g, d in fresh[step]:
                    part_copy(g, d).start()

    for copy in fac_copies:
        copy.wait()
    mask_group(1)
    store_parts(0, 0, sum_products(0, far_row, 2 * SLAB, 0, AUX))
    send_parts(0)
    store_parts(1, 0, sum_products(1, far_row, 2 * SLAB, 0, AUX))
    send_parts(1)
    peer_row = pl.multiple_of(near_row + (1 - core) * SLAB, SLAB)
    own_row = pl.multiple_of(near_row + core * SLAB, SLAB)
    part[0, 1, 1 - core] = sum_products(0, peer_row, SLAB, 0, AUX)
    send_parts(2)
    part[0, 1, core] = sum_products(0, own_row, SLAB, 0, AUX)

    @pl.when(z // 4 == MEETS[0])
    def _():
        reduce_and_turn(0)

    part[1, 1, 1 - core] = sum_products(1, peer_row, SLAB, 0, AUX)
    send_parts(3)
    part[1, 1, core] = sum_products(1, own_row, SLAB, 0, AUX)

    @pl.when(z // 4 != MEETS[0])
    def _():
        reduce_and_turn(0)

    reduce_and_turn(1)
    forward(0)
    forward(1)

    row_ids = v * SLAB + lax.broadcasted_iota(jnp.int32, (SLAB, VIRT), 0)
    col_ids = lax.broadcasted_iota(jnp.int32, (SLAB, VIRT), 1)
    reach_out = jnp.maximum(row_ids, col_ids)
    for ks in range(2):
        for vs in range(4):
            pltpu.make_async_copy(
                mirror.at[vs, ks], mirror.at[vs, ks], mirror_recv.at[vs, ks]
            ).wait()
        pieces = [mirror[vs, ks] for vs in range(4)]
        for sl in range(2):
            for t in range(2):
                p_own, p_in = sl * 2 + t, t * 2 + sl
                flipped = jnp.zeros((SLAB, VIRT), jnp.float32)
                for vs in range(4):
                    turn = ((vs - p_in) % 4) * SLAB
                    moved = pltpu.roll(pieces[vs], turn, 1) if turn else pieces[vs]
                    flipped = jnp.where(col_ids // SLAB == vs, moved, flipped)
                s = 2 * ks + sl
                summed = own[ks, p_own * SLAB : (p_own + 1) * SLAB, :] + flipped
                limit = jnp.where(live[t, s] > 0, counts[t, s], 0)
                out[s, t] = jnp.where(reach_out < limit, summed, 0.0)

    for g in range(2):
        for d in (1, 2, 3):
            part_copy(g, d).wait_send()
    for h, vd, bx, dy in ROUTES:
        if bx or dy:
            relay_copy(h, vd, bx, dy).wait_send()
        here, remote, _ = last_leg(h, vd, bx, dy)

        @pl.when(jnp.logical_not(here))
        def _():
            remote().wait_send()


def on_device(amplitudes, factors, pno_counts, pair_live):
    arguments = (amplitudes, factors, pno_counts.T, pair_live.T)
    dma = pltpu.SemaphoreType.DMA
    tile = (4 * SLAB, VIRT)
    return pl.pallas_call(
        kernel,
        out_shape=jax.ShapeDtypeStruct((4, 2, SLAB, VIRT), jnp.float32),
        in_specs=[pl.BlockSpec(memory_space=pltpu.HBM)] * 4,
        out_specs=pl.BlockSpec(memory_space=pltpu.VMEM),
        scratch_shapes=[
            pltpu.SMEM((2, 4), jnp.int32),
            pltpu.SMEM((2, 4), jnp.int32),
            pltpu.VMEM((4, 2, VIRT, VIRT), jnp.bfloat16),
            pltpu.VMEM((AUX, VIRT, VIRT), jnp.bfloat16),
            pltpu.VMEM((2, VIRT, 4 * VIRT), jnp.bfloat16),
            pltpu.VMEM((2, 2, 2) + tile, jnp.float32),
            pltpu.VMEM((2, 3) + tile, jnp.float32),
            pltpu.VMEM((2,) + tile, jnp.float32),
            pltpu.VMEM((8, SLAB, VIRT), jnp.float32),
            pltpu.VMEM((8, SLAB, VIRT), jnp.float32),
            pltpu.VMEM((4, 2, SLAB, VIRT), jnp.float32),
            dma((2,)),
            dma,
            dma((LOADS,)),
            dma((2, 3)),
            dma((2, 3)),
            dma((8,)),
            dma((8,)),
            dma((8,)),
            dma((4, 2)),
        ],
        compiler_params=pltpu.CompilerParams(
            collective_id=0, has_side_effects=True, vmem_limit_bytes=48 << 20
        ),
        name="ladder",
    )(*(pltpu.with_memory_space_constraint(a, pltpu.HBM) for a in arguments))


def solution(mesh):
    in_specs = (
        P("row", "col", None, None),
        P("row", "col", "vc", None, None),
        P("row", "col"),
        P("row", "col"),
    )
    out_specs = P("row", "col", "vc", None)
    return jax.shard_map(
        on_device, mesh=mesh, in_specs=in_specs, out_specs=out_specs, check_vma=False
    )
```
